256 devices in a mesh: expert: 64 (over z, y, core), dp: 4 (over x).
Axes of the slice: x: 4, y: 4, z: 8, core: 2. Of those that a mesh axis runs over, the one named last changes fastest.
Arguments:
- tokens: bfloat16 [4, 8192, 2048], P('dp', 'expert'), may hold values from -6 to 6
- cotangent: bfloat16 [4, 8192, 2048], P('dp', 'expert'), may hold values from -6 to 6
- picks: int32 [4, 64, 256], P('dp', 'expert'), may hold values from 0 to 8191, as said below
- valid: int32 [4, 64, 256], P('dp', 'expert'), may hold values 0 or 1
- comb: float32 [4, 64, 256], P('dp', 'expert'), may hold values from 0.25 to 1
- w_in: bfloat16 [64, 2048, 1024], P('expert'), may hold values from -0.125 to 0.125
- w_out: bfloat16 [64, 1024, 2048], P('expert'), may hold values from -0.1875 to 0.1875
Outputs:
- mixed: bfloat16 [4, 8192, 2048], P('dp', 'expert')
- grad_tokens: bfloat16 [4, 8192, 2048], P('dp', 'expert')
- grad_in: bfloat16 [64, 2048, 1024], P('expert', 'dp')
- grad_out: bfloat16 [64, 1024, 2048], P('expert', None, 'dp')
The draws below stay inside these ranges and needn't reach their ends.
Inputs may be any that keep to these rules, and one draw needn't show every extreme that they name: `picks`: each slot names a token of its group; the 256 slots of one expert in one group name distinct tokens, and at most 8 of them name tokens of one device's 128; for every expert and group some device's tokens are named by exactly 8 slots. Padded slots name tokens like the others.
All inputs are finite; a program needn't handle non-finite values. No bound on the sum of `valid` on one device may be relied on, other than what follows from the above.
Results may differ from the reference program's by a relative error of at most 0.013.
Values may be sent and summed in bfloat16 or wider, within the bound.
A program may use at most 128 MiB of HBM per device.

```python
import math
from functools import partial
import jax
import jax.numpy as jnp
from jax import lax

D = 2048
FFW = 1024
TOK_DEV = 128
GROUPS = 4
EXPERTS = 64
GROUP = 8192
CAP = 256
MOST = 8


def draw_picks(key, part):
    key = jax.random.fold_in(key, 11)
    key_favored, key_bias, key_base, key_offset = jax.random.split(key, 4)
    owners = GROUP // TOK_DEV
    row_count = GROUPS * EXPERTS
    cells = owners * MOST
    favored = jax.random.randint(key_favored, (row_count, 1), 0, owners)
    owner_bias = jax.random.randint(key_bias, (row_count, owners), 0, 4)
    owner_ids = jnp.arange(owners, dtype=jnp.int32)[None, :]
    owner_bias = jnp.where(owner_ids == favored, 8, owner_bias)
    base_score = jax.random.randint(key_base, (row_count, cells), 0, 4096)
    cell_ids = jnp.arange(cells, dtype=jnp.int32)
    cell_owner = cell_ids // MOST
    score = (jnp.take(owner_bias, cell_owner, axis=1) * 1024 + base_score) * cells + cell_ids[None, :]
    unused, chosen = lax.top_k(score, CAP)
    chosen_owner = chosen // MOST
    chosen_rank = chosen % MOST
    offsets = jax.random.randint(key_offset, (row_count, owners), 0, TOK_DEV)
    start_row = jnp.take_along_axis(offsets, chosen_owner, axis=1)
    local_row = (start_row + chosen_rank) % TOK_DEV
    return (chosen_owner * TOK_DEV + local_row).reshape(GROUPS, EXPERTS, CAP).astype(jnp.int32)


def place_ends(array, own_key, least, high):
    longest = array.shape.index(max(array.shape))
    spots = []
    for shift in (0, 1):
        where = [jax.random.randint(jax.random.fold_in(own_key, axis), (), 0, length) for axis, length in enumerate(array.shape)]
        where[longest] = (where[longest] + shift) % array.shape[longest]
        spots.append(tuple(where))
    return array.at[spots[0]].set(least).at[spots[1]].set(high)


def level_of(own_key, extent, cuts, low, top_value):
    factor_of = 1.0
    for position, shards_of in cuts:
        draws = jax.random.uniform(jax.random.fold_in(jax.random.fold_in(own_key, 6), position), (shards_of,), jnp.float32, low / len(cuts), top_value / len(cuts))
        factor_of = factor_of * jnp.repeat(jnp.exp(draws), extent[position] // shards_of).reshape((-1,) + (1,) * (len(extent) - 1 - position))
    return factor_of


def gaussian(own_key, extent, scale, limit, pieces=(), kind=jnp.bfloat16):
    factor_of = level_of(own_key, extent, pieces, -0.22, 0.18) if pieces else 1.0
    entries = jax.random.normal(own_key, extent, jnp.float32) * scale * factor_of
    return jnp.minimum(jnp.maximum(entries, -limit), limit).astype(kind)


def setup_inputs(seed: int = 0) -> dict:
    arg_keys = jax.random.split(jax.random.key(seed), 8)
    tokens = gaussian(arg_keys[0], (GROUPS, GROUP, D), 1.0, 6.0, ((0, 4), (1, 64)))
    cotangent = gaussian(arg_keys[1], (GROUPS, GROUP, D), 1.0, 6.0, ((0, 4), (1, 64)))
    picks = draw_picks(jax.random.fold_in(arg_keys[7], 71), 0)
    valid = place_ends((jax.random.randint(arg_keys[3], (GROUPS, EXPERTS, CAP), 0, 8) < 7).astype(jnp.int32), jax.random.fold_in(arg_keys[3], 1), 0, 1)
    comb = jnp.clip(jnp.exp(math.log(1.0) - 1.3862944 * jax.random.uniform(arg_keys[4], (GROUPS, EXPERTS, CAP), jnp.float32) ** level_of(arg_keys[4], (GROUPS, EXPERTS, CAP), ((0, 4), (1, 64)), -0.2, 0.2)), 0.25, 1.0)
    w_in = gaussian(arg_keys[5], (EXPERTS, D, FFW), D ** -0.5, 0.125, ((0, 64),))
    w_out = gaussian(arg_keys[6], (EXPERTS, FFW, D), FFW ** -0.5, 0.1875, ((0, 64),))
    return {"tokens": tokens, "cotangent": cotangent, "picks": picks, "valid": valid, "comb": comb, "w_in": w_in, "w_out": w_out}


def gelu_pair(pre_act):
    return jax.vjp(partial(jax.nn.gelu, approximate=True), pre_act)

def expert_group(token_block, cot_block, slot_rows, slot_scale, weight_in, weight_out):
    token_in = jnp.take(token_block, slot_rows, axis=0)
    pre_act = jnp.dot(token_in, weight_in, preferred_element_type=jnp.float32)
    act_value, act_back = gelu_pair(pre_act)
    hidden = act_value.astype(jnp.bfloat16)
    expert_out = jnp.dot(hidden, weight_out, preferred_element_type=jnp.float32)
    contrib = (slot_scale[:, None] * expert_out).astype(jnp.bfloat16)
    cot_in = jnp.take(cot_block, slot_rows, axis=0)
    d_out = (slot_scale[:, None] * cot_in.astype(jnp.float32)).astype(jnp.bfloat16)
    d_hidden = jnp.dot(d_out, weight_out.T, preferred_element_type=jnp.float32)
    d_pre = act_back(d_hidden)[0].astype(jnp.bfloat16)
    d_token = jnp.dot(d_pre, weight_in.T, preferred_element_type=jnp.float32).astype(jnp.bfloat16)
    part_in = jnp.dot(token_in.T, d_pre, preferred_element_type=jnp.float32).astype(jnp.bfloat16)
    part_out = jnp.dot(hidden.T, d_out, preferred_element_type=jnp.float32).astype(jnp.bfloat16)
    return (contrib, d_token, part_in, part_out)

def reference(tokens, cotangent, picks, valid, comb, w_in, w_out):
    scales = comb * valid.astype(jnp.float32)

    def per_expert(state_pair, inputs):
        mixed_acc, grad_acc = state_pair
        slot_table, scale_table, weight_in, weight_out = inputs
        total_in = jnp.zeros(weight_in.shape, jnp.float32)
        total_out = jnp.zeros(weight_out.shape, jnp.float32)
        for group_id in range(GROUPS):
            slot_rows = slot_table[group_id].astype(jnp.int32)
            results = expert_group(tokens[group_id], cotangent[group_id], slot_rows, scale_table[group_id], weight_in, weight_out)
            contrib, d_token, part_in, part_out = lax.optimization_barrier(results)
            mixed_acc = mixed_acc.at[group_id, slot_rows].add(contrib.astype(jnp.float32))
            grad_acc = grad_acc.at[group_id, slot_rows].add(d_token.astype(jnp.float32))
            total_in = total_in + part_in.astype(jnp.float32)
            total_out = total_out + part_out.astype(jnp.float32)
        return ((mixed_acc, grad_acc), (total_in.astype(jnp.bfloat16), total_out.astype(jnp.bfloat16)))
    start = (jnp.zeros(tokens.shape, jnp.float32), jnp.zeros(tokens.shape, jnp.float32))
    stacked = (jnp.swapaxes(picks, 0, 1), jnp.swapaxes(scales, 0, 1), w_in, w_out)
    (mixed_acc, grad_acc), (grad_in, grad_out) = lax.scan(per_expert, start, stacked)
    return (mixed_acc.astype(jnp.bfloat16), grad_acc.astype(jnp.bfloat16), grad_in, grad_out)
```

```python
from functools import partial

import jax
import jax.numpy as jnp
from jax import lax
from jax.experimental import pallas as pl
from jax.experimental.pallas import tpu as pltpu
from jax.sharding import PartitionSpec as P

MESH = pl.DeviceIdType.MESH
PLANE = 8
MOST = 8
TIGHT = 304
VMEM = pl.BlockSpec(memory_space=pltpu.VMEM)
BF = jnp.bfloat16
F32 = jnp.float32
I32 = jnp.int32


def dot(a, b):
    return jnp.dot(a, b, preferred_element_type=F32)


def one(mask):
    return jnp.where(mask, 1.0, 0.0).astype(BF)


def iota(shape, dim):
    return lax.broadcasted_iota(I32, shape, dim)


class Place:
    def __init__(self, planes, groups):
        self.planes, self.groups = planes, groups
        index = lax.axis_index("expert")
        self.z, self.k, self.x = index // PLANE, index % PLANE, lax.axis_index("dp")

    def mate(self, d):
        spot = lax.rem(self.k + d, PLANE)
        return spot, (self.z * PLANE + spot, self.x)

    def above(self, d):
        spot = lax.rem(self.z + d, self.planes)
        return spot, (spot * PLANE + self.k, self.x)

    def group(self, d):
        spot = lax.rem(self.x + d, self.groups)
        return spot, (self.z * PLANE + self.k, spot)

    def greet(self):
        barrier = pltpu.get_barrier_semaphore()
        peers = [self.mate(d)[1] for d in range(1, PLANE)]
        peers += [self.above(d)[1] for d in range(1, self.planes)]
        peers += [self.group(d)[1] for d in range(1, self.groups)]
        for peer in peers:
            pl.semaphore_signal(barrier, inc=1, device_id=peer, device_id_type=MESH)
        pl.semaphore_wait(barrier, len(peers))


def remote(src, dst, send, recv, peer):
    return pltpu.make_async_remote_copy(
        src_ref=src, dst_ref=dst, send_sem=send, recv_sem=recv, device_id=peer, device_id_type=MESH
    )


def far_first(i, count):
    half, sign = (i + 1) // 2, 2 * lax.rem(i, 2) - 1
    return lax.rem(count // 2 + sign * half, count)


def block(index, size):
    return pl.ds(pl.multiple_of(index * size, size), size)


def loop(low, high, step):
    def run(i, carry):
        step(i)
        return carry

    lax.fori_loop(low, high, run, 0)


def dispatch_kernel(
    planes, groups, cap,
    tok_ref, cot_ref, picks_ref,
    tin_ref, cin_ref, row_ref, rank_ref, flag_ref,
    picks_all, maps, flags, rows_pad, tall, pool, packed, hot, pick_hot, got, parts,
    pick_sem, map_sem, flag_sem, pool_sem, z_sem, part_sem, own_sem,
):
    me = Place(planes, groups)
    z, k, x = me.z, me.k, me.x
    tok, model = tok_ref.shape
    slots = picks_ref.shape[1]
    width = model // PLANE
    n_dev = planes * PLANE
    all_slots = PLANE * slots
    me.greet()

    def pick_copy(d):
        return remote(picks_ref, picks_all.at[k], pick_sem.at[0, d], pick_sem.at[1, d], me.mate(d)[1])

    def pool_copy(which, d):
        spot, peer = me.mate(d)
        return remote(
            (tok_ref, cot_ref)[which].at[:, block(spot, width)],
            pool.at[which, block(k, tok)],
            pool_sem.at[0, which, d], pool_sem.at[1, which, d], peer,
        )

    for d in range(1, PLANE):
        pick_copy(d).start()
    for which in range(2):
        for d in range(1, PLANE):
            pool_copy(which, d).start()
    own = [
        pltpu.make_async_copy(
            (tok_ref, cot_ref)[which].at[:, block(k, width)], pool.at[which, block(k, tok)], own_sem.at[which]
        )
        for which in range(2)
    ]
    for copy in own:
        copy.start()
    picks_all[k] = picks_ref[...]
    for d in range(1, PLANE):
        pick_copy(d).wait_recv()

    names = jnp.concatenate([picks_all[i] for i in range(PLANE)], axis=1)
    high, low = names // tok, lax.rem(names, tok)
    high_hot = iota((n_dev, all_slots), 0) == high
    low_hot = one(iota((tok, all_slots), 0) == low)
    tall[...] = low_hot
    count = lax.dot_general(
        one(high_hot), low_hot, (((1,), (1,)), ((), ())), preferred_element_type=F32
    )
    need = count > 0.5
    need_one = one(need)
    before = one(iota((tok, tok), 0) < iota((tok, tok), 1))
    row_a, row_b = iota((n_dev, n_dev), 0), iota((n_dev, n_dev), 1)
    earlier = one((row_b < row_a) & (row_b // PLANE == row_a // PLANE))
    rank = dot(need_one, before) + jnp.sum(dot(earlier, need_one), axis=1, keepdims=True)
    over = jnp.max(jnp.where(need & (rank > cap - 0.5), 1, 0), axis=(0, 1), keepdims=True)
    ranked = jnp.where(need, rank.astype(I32), -1)
    for p in range(planes):
        maps[p, 0:PLANE] = ranked[p * PLANE : (p + 1) * PLANE]
        maps[p, PLANE : 2 * PLANE] = jnp.broadcast_to(over, (PLANE, tok))

    def map_copy(d):
        spot, peer = me.above(d)
        return remote(maps.at[spot], rank_ref.at[z], map_sem.at[0, d], map_sem.at[1, d], peer)

    for d in range(1, planes):
        map_copy(d).start()
    rank_ref[z] = maps[z]

    rank_hi = jnp.floor(rank * (1.0 / 32.0))
    rank_lo = rank - 32.0 * rank_hi
    found = 32.0 * dot(rank_hi.astype(BF), tall[...]) + dot(rank_lo.astype(BF), tall[...])
    slot_rank = jnp.sum(jnp.where(high_hot, found, 0.0), axis=0, keepdims=True).astype(I32)
    slot_row = jnp.where(slot_rank < cap, (high // PLANE) * cap + slot_rank, -1)
    row_ref[...] = slot_row

    for d in range(1, planes):
        map_copy(d).wait_recv()
    over_group = jnp.max(rank_ref[:, PLANE : 2 * PLANE, :], axis=0)
    flags[x] = over_group

    def flag_copy(d):
        return remote(flags.at[x], flags.at[x], flag_sem.at[0, d], flag_sem.at[1, d], me.group(d)[1])

    for d in range(1, groups):
        flag_copy(d).start()

    def z_copy(which, d):
        return remote(
            packed.at[which, d], got.at[which, block(z, cap)],
            z_sem.at[0, which, d], z_sem.at[1, which, d], me.above(d)[1],
        )

    def fill_hot(d):
        spot = lax.rem(z + d, planes)
        rank_map = rank_ref[spot, 0:PLANE]
        for h in range(PLANE):
            hot[d, :, h * tok : (h + 1) * tok] = one(iota((cap, tok), 0) == rank_map[h : h + 1, :])

    def pack(which, d):
        return dot(hot[d], pool[which]).astype(BF)

    def send_tokens(i):
        d = far_first(i, planes)
        fill_hot(d)
        packed[0, d] = pack(0, d)
        z_copy(0, d).start()

    own[0].wait()
    for d in range(1, PLANE):
        pool_copy(0, d).wait_recv()
    loop(0, planes - 1, send_tokens)
    fill_hot(0)
    got[0, block(z, cap)] = pack(0, 0)

    def send_cots(i):
        d = far_first(i, planes)
        packed[1, d] = pack(1, d)
        z_copy(1, d).start()

    own[1].wait()
    for d in range(1, PLANE):
        pool_copy(1, d).wait_recv()
    loop(0, planes - 1, send_cots)
    got[1, block(z, cap)] = pack(1, 0)

    for b in range(all_slots // tok):
        rows_pad[b : b + 1, :] = slot_row[:, b * tok : (b + 1) * tok].astype(F32)
    turned = rows_pad[...].T.astype(I32)
    for b in range(all_slots // tok):
        pick_hot[b * tok : (b + 1) * tok, :] = one(
            iota((tok, planes * cap), 1) == turned[:, b : b + 1]
        )

    def part_copy(which, d):
        return remote(
            parts.at[which, d], (tin_ref, cin_ref)[which].at[:, block(k, width)],
            part_sem.at[0, which, d], part_sem.at[1, which, d], me.mate(d)[1],
        )

    for which in range(2):
        for d in range(1, planes):
            z_copy(which, d).wait_recv()

        def select(d, which=which):
            spot = lax.rem(k + d, PLANE)
            parts[which, d] = dot(pick_hot[block(spot, slots)], got[which]).astype(BF)

        def select_send(d, which=which):
            select(d)
            part_copy(which, d).start()

        loop(1, PLANE, select_send)
        select(0)
        home = pltpu.make_async_copy(
            parts.at[which, 0], (tin_ref, cin_ref)[which].at[:, block(k, width)], own_sem.at[which]
        )
        home.start()
        home.wait()

    for d in range(1, groups):
        flag_copy(d).wait()
    flag_ref[...] = jnp.max(flags[...], axis=0)
    for which in range(2):
        for d in range(1, PLANE):
            part_copy(which, d).wait()
            pool_copy(which, d).wait_send()
        for d in range(1, planes):
            z_copy(which, d).wait_send()
    for d in range(1, PLANE):
        pick_copy(d).wait_send()
    for d in range(1, planes):
        map_copy(d).wait_send()


def dispatch(planes, groups, cap, ident, tokens, cotangent, picks):
    tok, model = tokens.shape
    slots = picks.shape[1]
    width = model // PLANE
    all_slots = PLANE * slots
    dma = pltpu.SemaphoreType.DMA
    return pl.pallas_call(
        partial(dispatch_kernel, planes, groups, cap),
        out_shape=(
            jax.ShapeDtypeStruct((slots, model), BF),
            jax.ShapeDtypeStruct((slots, model), BF),
            jax.ShapeDtypeStruct((1, all_slots), I32),
            jax.ShapeDtypeStruct((planes, 2 * PLANE, tok), I32),
            jax.ShapeDtypeStruct((PLANE, tok), I32),
        ),
        in_specs=[VMEM] * 3,
        out_specs=[VMEM] * 5,
        scratch_shapes=[
            pltpu.VMEM((PLANE, 1, slots), I32),
            pltpu.VMEM((planes, 2 * PLANE, tok), I32),
            pltpu.VMEM((groups, PLANE, tok), I32),
            pltpu.VMEM((tok, tok), F32),
            pltpu.VMEM((tok, all_slots), BF),
            pltpu.VMEM((2, PLANE * tok, width), BF),
            pltpu.VMEM((2, planes, cap, width), BF),
            pltpu.VMEM((planes, cap, PLANE * tok), BF),
            pltpu.VMEM((all_slots, planes * cap), BF),
            pltpu.VMEM((2, planes * cap, width), BF),
            pltpu.VMEM((2, PLANE, slots, width), BF),
            dma((2, PLANE)),
            dma((2, planes)),
            dma((2, groups)),
            dma((2, 2, PLANE)),
            dma((2, 2, planes)),
            dma((2, 2, PLANE)),
            dma((2,)),
        ],
        compiler_params=pltpu.CompilerParams(
            collective_id=ident, has_side_effects=True, vmem_limit_bytes=60 * 2**20
        ),
        name=f"dispatch_{cap}",
    )(tokens, cotangent, picks)


def combine_kernel(
    planes, groups, cap,
    con_ref, dtk_ref, row_ref, rank_ref, tin_ref, dout_ref, hid_ref, dpre_ref,
    mixed_ref, gtok_ref, tins_ref, douts_ref, hids_ref, dpres_ref,
    msgs, row_hot, sums, got, ranks_pad, back_hot, final,
    msg_sem, z_sem, final_sem, x_sem, own_sem,
):
    me = Place(planes, groups)
    z, k, x = me.z, me.k, me.x
    slots, model = con_ref.shape
    tok = mixed_ref.shape[0]
    width = model // PLANE
    all_slots = PLANE * slots
    stride = got.shape[1] // planes
    part = model // groups
    me.greet()

    def msg_copy(which, d):
        spot, peer = me.mate(d)
        return remote(
            (con_ref, dtk_ref)[which].at[:, block(spot, width)], msgs.at[which, block(k, slots)],
            msg_sem.at[0, which, d], msg_sem.at[1, which, d], peer,
        )

    def x_copy(which, d):
        spot, peer = me.group(d)
        src = (
            hid_ref, dpre_ref, tin_ref.at[:, block(spot, part)], dout_ref.at[:, block(spot, part)]
        )[which]
        dst = (hids_ref, dpres_ref, tins_ref, douts_ref)[which].at[x]
        return remote(src, dst, x_sem.at[0, which, d], x_sem.at[1, which, d], peer)

    own = []
    for which in range(2):
        for d in range(1, PLANE):
            msg_copy(which, d).start()
        own.append(
            pltpu.make_async_copy(
                (con_ref, dtk_ref)[which].at[:, block(k, width)], msgs.at[which, block(k, slots)],
                own_sem.at[which],
            )
        )
    for which in range(4):
        for d in range(1, groups):
            x_copy(which, d).start()
        src = (hid_ref, dpre_ref, tin_ref.at[:, block(x, part)], dout_ref.at[:, block(x, part)])[which]
        dst = (hids_ref, dpres_ref, tins_ref, douts_ref)[which].at[x]
        own.append(pltpu.make_async_copy(src, dst, own_sem.at[2 + which]))
    for copy in own:
        copy.start()

    def z_copy(which, d):
        return remote(
            sums.at[which, d],
            got.at[which, pl.ds(pl.multiple_of(z * stride, stride), cap)],
            z_sem.at[0, which, d], z_sem.at[1, which, d], me.above(d)[1],
        )

    def fill(d):
        spot = lax.rem(z + d, planes)
        row_hot[d] = one(iota((cap, all_slots), 0) + spot * cap == row_ref[...])

    def add_up(which, d):
        return dot(row_hot[d], msgs[which]).astype(BF)

    for which in range(2):
        if which == 0:
            fill(0)
        own[which].wait()
        for d in range(1, PLANE):
            msg_copy(which, d).wait_recv()

        def send_sums(i, which=which):
            d = far_first(i, planes)
            if which == 0:
                fill(d)
            sums[which, d] = add_up(which, d)
            z_copy(which, d).start()

        loop(0, planes - 1, send_sums)
        got[which, pl.ds(pl.multiple_of(z * stride, stride), cap)] = add_up(which, 0)

    if stride > cap:
        for which in range(2):
            for p in range(planes):
                got[which, p * stride + cap : (p + 1) * stride] = jnp.zeros((stride - cap, width), BF)

    for p in range(planes):
        ranks_pad[p * PLANE : (p + 1) * PLANE] = rank_ref[p, 0:PLANE].astype(F32)
    turned = ranks_pad[...].T.astype(I32)
    for h in range(PLANE):
        for p in range(planes):
            c = p * PLANE + h
            back_hot[h * tok : (h + 1) * tok, p * stride : (p + 1) * stride] = one(
                iota((tok, stride), 1) == turned[:, c : c + 1]
            )

    def final_copy(which, d):
        return remote(
            final.at[which, d], (mixed_ref, gtok_ref)[which].at[:, block(k, width)],
            final_sem.at[0, which, d], final_sem.at[1, which, d], me.mate(d)[1],
        )

    for which in range(2):
        for d in range(1, planes):
            z_copy(which, d).wait_recv()

        def total(d, which=which):
            spot = lax.rem(k + d, PLANE)
            final[which, d] = dot(back_hot[block(spot, tok)], got[which]).astype(BF)

        def total_send(d, which=which):
            total(d)
            final_copy(which, d).start()

        loop(1, PLANE, total_send)
        total(0)
        home = pltpu.make_async_copy(
            final.at[which, 0], (mixed_ref, gtok_ref)[which].at[:, block(k, width)], own_sem.at[which]
        )
        home.start()
        home.wait()

    for which in range(2):
        for d in range(1, PLANE):
            final_copy(which, d).wait()
            msg_copy(which, d).wait_send()
        for d in range(1, planes):
            z_copy(which, d).wait_send()
    for which in range(4):
        own[2 + which].wait()
        for d in range(1, groups):
            x_copy(which, d).wait()


def combine(planes, groups, cap, ident, contrib, d_token, row, rank, token_in, d_out, hidden, d_pre):
    slots, model = contrib.shape
    tok = rank.shape[2]
    width = model // PLANE
    all_slots = PLANE * slots
    stride = -(-cap // 128) * 128
    dma = pltpu.SemaphoreType.DMA
    return pl.pallas_call(
        partial(combine_kernel, planes, groups, cap),
        out_shape=(
            jax.ShapeDtypeStruct((tok, model), BF),
            jax.ShapeDtypeStruct((tok, model), BF),
            jax.ShapeDtypeStruct((groups, slots, model // groups), BF),
            jax.ShapeDtypeStruct((groups, slots, model // groups), BF),
            jax.ShapeDtypeStruct((groups,) + hidden.shape, BF),
            jax.ShapeDtypeStruct((groups,) + d_pre.shape, BF),
        ),
        in_specs=[VMEM] * 8,
        out_specs=[VMEM] * 6,
        scratch_shapes=[
            pltpu.VMEM((2, all_slots, width), BF),
            pltpu.VMEM((planes, cap, all_slots), BF),
            pltpu.VMEM((2, planes, cap, width), BF),
            pltpu.VMEM((2, planes * stride, width), BF),
            pltpu.VMEM((tok, tok), F32),
            pltpu.VMEM((PLANE * tok, planes * stride), BF),
            pltpu.VMEM((2, PLANE, tok, width), BF),
            dma((2, 2, PLANE)),
            dma((2, 2, planes)),
            dma((2, 2, PLANE)),
            dma((2, 4, groups)),
            dma((6,)),
        ],
        compiler_params=pltpu.CompilerParams(
            collective_id=ident, has_side_effects=True, vmem_limit_bytes=60 * 2**20
        ),
        name=f"combine_{cap}",
    )(contrib, d_token, row, rank, token_in, d_out, hidden, d_pre)


def gelu_pair(pre_act):
    return jax.vjp(partial(jax.nn.gelu, approximate=True), pre_act)


def body(tokens, cotangent, picks, valid, comb, w_in, w_out):
    planes = lax.axis_size("expert") // PLANE
    groups = lax.axis_size("dp")
    loose = PLANE * min(tokens.shape[1], PLANE * MOST)
    names = picks[0]
    sent = dispatch(planes, groups, TIGHT, 0, tokens[0], cotangent[0], names)
    over = jnp.max(sent[4]) > 0
    token_in, cot_in, row, rank = lax.cond(
        over,
        lambda: tuple(dispatch(planes, groups, loose, 1, tokens[0], cotangent[0], names)[:4]),
        lambda: tuple(sent[:4]),
    )
    slot_scale = (comb[0, 0] * valid[0, 0].astype(F32))[:, None]
    pre_act = dot(token_in, w_in[0])
    act_value, act_back = gelu_pair(pre_act)
    hidden = act_value.astype(BF)
    contrib = (slot_scale * dot(hidden, w_out[0])).astype(BF)
    d_out = (slot_scale * cot_in.astype(F32)).astype(BF)
    d_hidden = lax.dot_general(d_out, w_out[0], (((1,), (1,)), ((), ())), preferred_element_type=F32)
    d_pre = act_back(d_hidden)[0].astype(BF)
    d_token = lax.dot_general(
        d_pre, w_in[0], (((1,), (1,)), ((), ())), preferred_element_type=F32
    ).astype(BF)
    operands = (contrib, d_token, row, rank, token_in, d_out, hidden, d_pre)
    mixed, grad_tokens, tins, douts, hids, dpres = lax.cond(
        over,
        lambda *a: tuple(combine(planes, groups, loose, 3, *a)),
        lambda *a: tuple(combine(planes, groups, TIGHT, 2, *a)),
        *operands,
    )
    over_rows = (((0, 1), (0, 1)), ((), ()))
    grad_in = lax.dot_general(tins, dpres, over_rows, preferred_element_type=F32).astype(BF)
    grad_out = lax.dot_general(hids, douts, over_rows, preferred_element_type=F32).astype(BF)
    return (mixed[None], grad_tokens[None], grad_in[None], grad_out[None])


def solution(mesh):
    placed = (
        P("dp", "expert", None),
        P("dp", "expert", None),
        P("dp", "expert", None),
        P("dp", "expert", None),
        P("dp", "expert", None),
        P("expert", None, None),
        P("expert", None, None),
    )
    return jax.shard_map(
        body,
        mesh=mesh,
        in_specs=placed,
        out_specs=(
            P("dp", "expert", None),
            P("dp", "expert", None),
            P("expert", "dp", None),
            P("expert", None, "dp"),
        ),
        check_vma=False,
    )
```

```python
from functools import partial

import jax
import jax.numpy as jnp
from jax import lax
from jax.experimental import pallas as pl
from jax.experimental.pallas import tpu as pltpu
from jax.sharding import PartitionSpec as P

MESH = pl.DeviceIdType.MESH
PLANE = 8
MOST = 8
LIMIT = 63
TIGHT = 304
VMEM = pl.BlockSpec(memory_space=pltpu.VMEM)
BF = jnp.bfloat16
F32 = jnp.float32
I32 = jnp.int32


def dot(a, b):
    return jnp.dot(a, b, preferred_element_type=F32)


def one(mask):
    return jnp.where(mask, 1.0, 0.0).astype(BF)


def iota(shape, dim):
    return lax.broadcasted_iota(I32, shape, dim)


class Place:
    def __init__(self, planes, groups):
        self.planes, self.groups = planes, groups
        index = lax.axis_index("expert")
        self.z, self.k, self.x = index // PLANE, index % PLANE, lax.axis_index("dp")

    def mate(self, d):
        spot = lax.rem(self.k + d, PLANE)
        return spot, (self.z * PLANE + spot, self.x)

    def above(self, d):
        spot = lax.rem(self.z + d, self.planes)
        return spot, (spot * PLANE + self.k, self.x)

    def group(self, d):
        spot = lax.rem(self.x + d, self.groups)
        return spot, (self.z * PLANE + self.k, spot)

    def greet(self):
        barrier = pltpu.get_barrier_semaphore()
        peers = [self.mate(d)[1] for d in range(1, PLANE)]
        peers += [self.above(d)[1] for d in range(1, self.planes)]
        peers += [self.group(d)[1] for d in range(1, self.groups)]
        for peer in peers:
            pl.semaphore_signal(barrier, inc=1, device_id=peer, device_id_type=MESH)
        pl.semaphore_wait(barrier, len(peers))


def remote(src, dst, send, recv, peer):
    return pltpu.make_async_remote_copy(
        src_ref=src, dst_ref=dst, send_sem=send, recv_sem=recv, device_id=peer, device_id_type=MESH
    )


def far_first(i, count):
    half, sign = (i + 1) // 2, 2 * lax.rem(i, 2) - 1
    return lax.rem(count // 2 + sign * half, count)


def block(index, size):
    return pl.ds(pl.multiple_of(index * size, size), size)


def dot_nt(a, b):
    return lax.dot_general(a, b, (((1,), (1,)), ((), ())), preferred_element_type=F32)


def dot_tn(a, b):
    return lax.dot_general(a, b, (((0,), (0,)), ((), ())), preferred_element_type=F32)


def loop(low, high, step):
    def run(i, carry):
        step(i)
        return carry

    lax.fori_loop(low, high, run, 0)


def layer_kernel(
    planes, groups, cap, stored,
    tok_ref, cot_ref, picks_ref, scale_ref, w_in_ref, w_out_ref,
    mixed_ref, gtok_ref, gin_ref, gout_ref, flag_ref,
    picks_all, maps, ranks, flags, turn, slot_cols, back_cols, tall, pool, hot, packed, pick_hot, got,
    parts, taken, wi, wo, pre, slope, hid, d_pre, msgs, row_hot, home, back_hot, final,
    tins, douts, hids, dpres, rows,
    pick_sem, map_sem, flag_sem, pool_sem, z_sem, part_sem, msg_sem, back_sem, final_sem, x_sem, own_sem,
):
    me = Place(planes, groups)
    z, k, x = me.z, me.k, me.x
    tok, model = tok_ref.shape
    slots = picks_ref.shape[1]
    width = model // PLANE
    n_dev = planes * PLANE
    all_slots = PLANE * slots
    stride = home.shape[1] // planes
    per_group = PLANE // groups
    ffw = hid.shape[1]
    me.greet()

    def pick_copy(d):
        return remote(picks_ref, picks_all.at[k], pick_sem.at[0, d], pick_sem.at[1, d], me.mate(d)[1])

    def pool_copy(which, d):
        spot, peer = me.mate(d)
        return remote(
            (tok_ref, cot_ref)[which].at[:, block(spot, width)],
            pool.at[which, block(k, tok)],
            pool_sem.at[0, which, d], pool_sem.at[1, which, d], peer,
        )

    def map_copy(d):
        spot, peer = me.above(d)
        return remote(maps.at[spot], ranks.at[z], map_sem.at[0, d], map_sem.at[1, d], peer)

    def flag_copy(d):
        return remote(flags.at[x], flags.at[x], flag_sem.at[0, d], flag_sem.at[1, d], me.group(d)[1])

    def z_copy(which, d):
        return remote(
            packed.at[which, d], got.at[which, block(z, cap)],
            z_sem.at[0, which, d], z_sem.at[1, which, d], me.above(d)[1],
        )

    def part_copy(which, d):
        return remote(
            parts.at[which, d], taken.at[which, k],
            part_sem.at[0, which, d], part_sem.at[1, which, d], me.mate(d)[1],
        )

    def msg_copy(which, d):
        return remote(
            parts.at[which, d], msgs.at[which, block(k, slots)],
            msg_sem.at[0, which, d], msg_sem.at[1, which, d], me.mate(d)[1],
        )

    def back_copy(which, d):
        return remote(
            packed.at[which, d],
            home.at[which, pl.ds(pl.multiple_of(z * stride, stride), cap)],
            back_sem.at[0, which, d], back_sem.at[1, which, d], me.above(d)[1],
        )

    def final_copy(which, d):
        return remote(
            final.at[which, d], (mixed_ref, gtok_ref)[which].at[:, block(k, width)],
            final_sem.at[0, which, d], final_sem.at[1, which, d], me.mate(d)[1],
        )

    def x_pair(which, spot):
        src = (
            hid, d_pre, taken.at[0, pl.ds(spot * per_group, per_group)],
            taken.at[1, pl.ds(spot * per_group, per_group)],
        )[which]
        return src, (hids, dpres, tins, douts)[which].at[x]

    def x_copy(which, d):
        spot, peer = me.group(d)
        src, dst = x_pair(which, spot)
        return remote(src, dst, x_sem.at[0, which, d], x_sem.at[1, which, d], peer)

    def x_own(which):
        src, dst = x_pair(which, x)
        return pltpu.make_async_copy(src, dst, own_sem.at[2 + which])

    def x_start(which):
        for d in range(1, groups):
            x_copy(which, d).start()
        x_own(which).start()

    for d in range(1, PLANE):
        pick_copy(d).start()
    for which in range(2):
        for d in range(1, PLANE):
            pool_copy(which, d).start()
    own = [
        pltpu.make_async_copy(
            (tok_ref, cot_ref)[which].at[:, block(k, width)], pool.at[which, block(k, tok)], own_sem.at[which]
        )
        for which in range(2)
    ]
    weights = [
        pltpu.make_async_copy(w_in_ref, wi, own_sem.at[6]),
        pltpu.make_async_copy(w_out_ref, wo, own_sem.at[7]),
    ]
    for copy in own + weights:
        copy.start()
    picks_all[k] = picks_ref[...]
    if stride > cap:
        for which in range(2):
            for p in range(planes):
                home[which, p * stride + cap : (p + 1) * stride] = jnp.zeros((stride - cap, width), BF)
    for d in range(1, PLANE):
        pick_copy(d).wait_recv()

    names = jnp.concatenate([picks_all[i] for i in range(PLANE)], axis=1)
    high, low = names // tok, lax.rem(names, tok)
    high_hot = iota((n_dev, all_slots), 0) == high
    low_hot = one(iota((tok, all_slots), 0) == low)
    tall[...] = low_hot
    need = dot_nt(one(high_hot), low_hot) > 0.5
    need_one = one(need)
    before = one(iota((tok, tok), 0) < iota((tok, tok), 1))
    row_a, row_b = iota((n_dev, n_dev), 0), iota((n_dev, n_dev), 1)
    earlier = one((row_b < row_a) & (row_b // PLANE == row_a // PLANE))
    rank = dot(need_one, before) + jnp.sum(dot(earlier, need_one), axis=1, keepdims=True)
    over = jnp.max(jnp.where(need & (rank > cap - 0.5), 1, 0), axis=(0, 1), keepdims=True)
    ranked = jnp.where(need, rank.astype(I32), -1)
    for p in range(planes):
        maps[p, 0:PLANE] = ranked[p * PLANE : (p + 1) * PLANE]
        maps[p, PLANE : 2 * PLANE] = jnp.broadcast_to(over, (PLANE, tok))
    for d in range(1, planes):
        map_copy(d).start()
    ranks[z] = maps[z]

    rank_hi = jnp.floor(rank * (1.0 / 32.0))
    rank_lo = rank - 32.0 * rank_hi
    found = 32.0 * dot(rank_hi.astype(BF), tall[...]) + dot(rank_lo.astype(BF), tall[...])
    slot_rank = jnp.sum(jnp.where(high_hot, found, 0.0), axis=0, keepdims=True).astype(I32)
    rows[...] = jnp.where(slot_rank < cap, (high // PLANE) * cap + slot_rank, -1)

    for d in range(1, planes):
        map_copy(d).wait_recv()
    flags[x] = jnp.max(ranks[:, PLANE : 2 * PLANE, :], axis=0)
    for d in range(1, groups):
        flag_copy(d).start()

    def pack(which, d, slot):
        rank_map = ranks[lax.rem(z + d, planes), 0:PLANE]
        for h in range(PLANE):
            hot[slot, :, h * tok : (h + 1) * tok] = one(iota((cap, tok), 0) == rank_map[h : h + 1, :])
        return dot(hot[slot], pool[which]).astype(BF)

    for which in range(2):
        own[which].wait()
        for d in range(1, PLANE):
            pool_copy(which, d).wait_recv()

        def send_rows(i, which=which):
            d = far_first(i, planes)
            packed[which, d] = pack(which, d, 0)
            z_copy(which, d).start()

        loop(0, planes - 1, send_rows)
        got[which, block(z, cap)] = pack(which, 0, 1)

    for b in range(all_slots // tok):
        turn[b : b + 1, :] = rows[:, b * tok : (b + 1) * tok].astype(F32)
    turned = turn[...].T.astype(I32)
    per = slots // tok
    for b in range(all_slots // tok):
        slot_cols[b // per, (b % per) * tok : (b % per + 1) * tok] = jnp.broadcast_to(
            turned[:, b : b + 1], (tok, tok)
        )

    def fill_pick(spot, slot):
        pick_hot[slot] = one(iota((slots, planes * cap), 1) == slot_cols[spot][:, 0:1])

    if stored:
        loop(0, PLANE, lambda spot: fill_pick(spot, spot))

    def select_all(which):
        for d in range(1, planes):
            z_copy(which, d).wait_recv()

        def select(d):
            spot = lax.rem(k + d, PLANE)
            if not stored:
                fill_pick(spot, 0)
            return dot(pick_hot[spot if stored else 0], got[which]).astype(BF)

        def send(d):
            parts[which, d] = select(d)
            part_copy(which, d).start()

        loop(1, PLANE, send)
        taken[which, k] = select(0)

    def each_chunk(which, step):
        step(k, True)
        for d in range(1, PLANE):
            part_copy(which, d).wait_recv()
            step(lax.rem(k + PLANE - d, PLANE), False)

    select_all(0)
    for copy in weights:
        copy.wait()

    def project(c, first):
        term = dot(taken[0, c], wi[block(c, width)])
        pre[...] = term if first else pre[...] + term

    each_chunk(0, project)
    x_start(2)
    tile = 32

    def activate(i):
        v = pre[block(i, tile)]
        inner = 0.7978845608028654 * (v + 0.044715 * (v * v * v))
        t = jnp.tanh(inner)
        hid[block(i, tile)] = (0.5 * v * (1.0 + t)).astype(BF)
        bend = 0.7978845608028654 * (1.0 + 0.134145 * (v * v))
        slope[block(i, tile)] = 0.5 * (1.0 + t) + 0.5 * v * ((1.0 - t * t) * bend)

    loop(0, slots // tile, activate)
    x_start(0)
    scale = scale_ref[:, 0:1]

    def contribution(d):
        spot = lax.rem(k + d, PLANE)
        return (scale * dot(hid[...], wo[:, block(spot, width)])).astype(BF)

    def send_contribution(d):
        part_copy(0, d).wait_send()
        parts[0, d] = contribution(d)
        msg_copy(0, d).start()

    loop(1, PLANE, send_contribution)
    msgs[0, block(k, slots)] = contribution(0)

    select_all(1)

    def send_sums(which):
        for d in range(1, PLANE):
            msg_copy(which, d).wait_recv()

        def add_up(d, slot):
            spot = lax.rem(z + d, planes)
            row_hot[slot] = one(iota((cap, all_slots), 0) + spot * cap == rows[...])
            return dot(row_hot[slot], msgs[which]).astype(BF)

        def send(i):
            d = far_first(i, planes)
            z_copy(which, d).wait_send()
            packed[which, d] = add_up(d, 0)
            back_copy(which, d).start()

        loop(0, planes - 1, send)
        home[which, pl.ds(pl.multiple_of(z * stride, stride), cap)] = add_up(0, 1)

    send_sums(0)

    def pull_back(c, first):
        d_out = (scale * taken[1, c].astype(F32)).astype(BF)
        taken[1, c] = d_out
        term = dot_nt(d_out, wo[:, block(c, width)])
        pre[...] = term if first else pre[...] + term

    each_chunk(1, pull_back)

    def chain(i):
        d_pre[block(i, tile)] = (pre[block(i, tile)] * slope[block(i, tile)]).astype(BF)

    loop(0, slots // tile, chain)

    def token_grad(d):
        spot = lax.rem(k + d, PLANE)
        return dot_nt(d_pre[...], wi[block(spot, width)]).astype(BF)

    def send_token_grad(d):
        part_copy(1, d).wait_send()
        parts[1, d] = token_grad(d)
        msg_copy(1, d).start()

    loop(1, PLANE, send_token_grad)
    msgs[1, block(k, slots)] = token_grad(0)
    x_start(1)
    x_start(3)
    send_sums(1)

    for p in range(planes):
        for h in range(PLANE):
            turn[h * planes + p : h * planes + p + 1] = ranks[p, h : h + 1].astype(F32)
    turned_back = turn[...].T.astype(I32)
    for h in range(PLANE):
        back_cols[h, :, 0:planes] = turned_back[:, h * planes : (h + 1) * planes]

    def fill_back(spot, slot):
        cols = back_cols[spot]
        for p in range(planes):
            back_hot[slot, :, p * stride : (p + 1) * stride] = one(
                iota((tok, stride), 1) == cols[:, p : p + 1]
            )

    if stored:
        loop(0, PLANE, lambda spot: fill_back(spot, spot))

    def send_totals(which):
        for d in range(1, planes):
            back_copy(which, d).wait_recv()

        def total(d):
            spot = lax.rem(k + d, PLANE)
            if not stored:
                fill_back(spot, 0)
            final[which, d] = dot(back_hot[spot if stored else 0], home[which]).astype(BF)

        def send(d):
            total(d)
            final_copy(which, d).start()

        loop(1, PLANE, send)
        total(0)
        pltpu.make_async_copy(
            final.at[which, 0], (mixed_ref, gtok_ref)[which].at[:, block(k, width)], own_sem.at[which]
        ).start()

    send_totals(0)
    send_totals(1)

    for which in range(4):
        x_own(which).wait()
        for d in range(1, groups):
            x_copy(which, d).wait_recv()
    for h in range(per_group):
        total_in = dot_tn(tins[0, h], dpres[0])
        for g in range(1, groups):
            total_in += dot_tn(tins[g, h], dpres[g])
        gin_ref[h * width : (h + 1) * width] = total_in.astype(BF)

    def out_grad(m):
        for h in range(per_group):
            total_out = dot_tn(hids[0, :, block(m, width)], douts[0, h])
            for g in range(1, groups):
                total_out += dot_tn(hids[g, :, block(m, width)], douts[g, h])
            gout_ref[block(m, width), h * width : (h + 1) * width] = total_out.astype(BF)

    loop(0, ffw // width, out_grad)

    for d in range(1, groups):
        flag_copy(d).wait()
        for which in range(4):
            x_copy(which, d).wait_send()
    flag_ref[...] = jnp.max(flags[...], axis=0)
    for which in range(2):
        pltpu.make_async_copy(
            final.at[which, 0], (mixed_ref, gtok_ref)[which].at[:, block(k, width)], own_sem.at[which]
        ).wait()
        for d in range(1, PLANE):
            final_copy(which, d).wait()
            msg_copy(which, d).wait_send()
            pool_copy(which, d).wait_send()
        for d in range(1, planes):
            back_copy(which, d).wait_send()
    for d in range(1, PLANE):
        pick_copy(d).wait_send()
    for d in range(1, planes):
        map_copy(d).wait_send()


def layer(planes, groups, cap, stored, ident, tokens, cotangent, picks, scale, w_in, w_out):
    tok, model = tokens.shape
    slots = picks.shape[1]
    ffw = w_in.shape[1]
    width = model // PLANE
    all_slots = PLANE * slots
    stride = -(-cap // 128) * 128
    per_group = PLANE // groups
    keep = PLANE if stored else 1
    dma = pltpu.SemaphoreType.DMA
    return pl.pallas_call(
        partial(layer_kernel, planes, groups, cap, stored),
        out_shape=(
            jax.ShapeDtypeStruct((tok, model), BF),
            jax.ShapeDtypeStruct((tok, model), BF),
            jax.ShapeDtypeStruct((model // groups, ffw), BF),
            jax.ShapeDtypeStruct((ffw, model // groups), BF),
            jax.ShapeDtypeStruct((PLANE, tok), I32),
        ),
        in_specs=[VMEM] * 4 + [pl.BlockSpec(memory_space=pl.ANY)] * 2,
        out_specs=[VMEM] * 5,
        scratch_shapes=[
            pltpu.VMEM((PLANE, 1, slots), I32),
            pltpu.VMEM((planes, 2 * PLANE, tok), I32),
            pltpu.VMEM((planes, 2 * PLANE, tok), I32),
            pltpu.VMEM((groups, PLANE, tok), I32),
            pltpu.VMEM((tok, tok), F32),
            pltpu.VMEM((PLANE, slots, tok), I32),
            pltpu.VMEM((PLANE, tok, tok), I32),
            pltpu.VMEM((tok, all_slots), BF),
            pltpu.VMEM((2, PLANE * tok, width), BF),
            pltpu.VMEM((2, cap, PLANE * tok), BF),
            pltpu.VMEM((2, planes, cap, width), BF),
            pltpu.VMEM((keep, slots, planes * cap), BF),
            pltpu.VMEM((2, planes * cap, width), BF),
            pltpu.VMEM((2, PLANE, slots, width), BF),
            pltpu.VMEM((2, PLANE, slots, width), BF),
            pltpu.VMEM(w_in.shape, BF),
            pltpu.VMEM(w_out.shape, BF),
            pltpu.VMEM((slots, ffw), F32),
            pltpu.VMEM((slots, ffw), F32),
            pltpu.VMEM((slots, ffw), BF),
            pltpu.VMEM((slots, ffw), BF),
            pltpu.VMEM((2, all_slots, width), BF),
            pltpu.VMEM((2, cap, all_slots), BF),
            pltpu.VMEM((2, planes * stride, width), BF),
            pltpu.VMEM((keep, tok, planes * stride), BF),
            pltpu.VMEM((2, PLANE, tok, width), BF),
            pltpu.VMEM((groups, per_group, slots, width), BF),
            pltpu.VMEM((groups, per_group, slots, width), BF),
            pltpu.VMEM((groups, slots, ffw), BF),
            pltpu.VMEM((groups, slots, ffw), BF),
            pltpu.VMEM((1, all_slots), I32),
            dma((2, PLANE)),
            dma((2, planes)),
            dma((2, groups)),
            dma((2, 2, PLANE)),
            dma((2, 2, planes)),
            dma((2, 2, PLANE)),
            dma((2, 2, PLANE)),
            dma((2, 2, planes)),
            dma((2, 2, PLANE)),
            dma((2, 4, groups)),
            dma((8,)),
        ],
        compiler_params=pltpu.CompilerParams(
            collective_id=ident, has_side_effects=True, vmem_limit_bytes=LIMIT * 2**20
        ),
        name=f"layer_{cap}",
    )(tokens, cotangent, picks, scale, w_in, w_out)


def body(tokens, cotangent, picks, valid, comb, w_in, w_out):
    planes = lax.axis_size("expert") // PLANE
    groups = lax.axis_size("dp")
    loose = PLANE * min(tokens.shape[1], PLANE * MOST)
    scale = comb[0, 0] * valid[0, 0].astype(F32)
    scale = jnp.broadcast_to(scale[:, None], (scale.shape[0], 128))
    operands = (tokens[0], cotangent[0], picks[0], scale, w_in[0], w_out[0])
    results = layer(planes, groups, TIGHT, True, 0, *operands)
    results = lax.cond(
        jnp.max(results[4]) > 0,
        lambda: tuple(layer(planes, groups, loose, False, 1, *operands)[:4]),
        lambda: tuple(results[:4]),
    )
    return tuple(result[None] for result in results)


def solution(mesh):
    placed = (
        P("dp", "expert", None),
        P("dp", "expert", None),
        P("dp", "expert", None),
        P("dp", "expert", None),
        P("dp", "expert", None),
        P("expert", None, None),
        P("expert", None, None),
    )
    return jax.shard_map(
        body,
        mesh=mesh,
        in_specs=placed,
        out_specs=(
            P("dp", "expert", None),
            P("dp", "expert", None),
            P("expert", "dp", None),
            P("expert", None, "dp"),
        ),
        check_vma=False,
    )
```

```python
from functools import partial

import jax
import jax.numpy as jnp
from jax import lax
from jax.experimental import pallas as pl
from jax.experimental.pallas import tpu as pltpu
from jax.sharding import PartitionSpec as P

MESH = pl.DeviceIdType.MESH
PLANE = 8
MOST = 8
LIMIT = 63
TIGHT = 304
VMEM = pl.BlockSpec(memory_space=pltpu.VMEM)
BF = jnp.bfloat16
F32 = jnp.float32
I32 = jnp.int32


def dot(a, b):
    return jnp.dot(a, b, preferred_element_type=F32)


def one(mask):
    return jnp.where(mask, 1.0, 0.0).astype(BF)


def iota(shape, dim):
    return lax.broadcasted_iota(I32, shape, dim)


class Place:
    def __init__(self, planes, groups):
        self.planes, self.groups = planes, groups
        index = lax.axis_index("expert")
        self.z, self.k, self.x = index // PLANE, index % PLANE, lax.axis_index("dp")

    def mate(self, d):
        spot = lax.rem(self.k + d, PLANE)
        return spot, (self.z * PLANE + spot, self.x)

    def above(self, d):
        spot = lax.rem(self.z + d, self.planes)
        return spot, (spot * PLANE + self.k, self.x)

    def group(self, d):
        spot = lax.rem(self.x + d, self.groups)
        return spot, (self.z * PLANE + self.k, spot)

    def greet(self):
        barrier = pltpu.get_barrier_semaphore()
        peers = [self.mate(d)[1] for d in range(1, PLANE)]
        peers += [self.above(d)[1] for d in range(1, self.planes)]
        peers += [self.group(d)[1] for d in range(1, self.groups)]
        for peer in peers:
            pl.semaphore_signal(barrier, inc=1, device_id=peer, device_id_type=MESH)
        pl.semaphore_wait(barrier, len(peers))


def remote(src, dst, send, recv, peer):
    return pltpu.make_async_remote_copy(
        src_ref=src, dst_ref=dst, send_sem=send, recv_sem=recv, device_id=peer, device_id_type=MESH
    )


def far_first(i, count):
    half, sign = (i + 1) // 2, 2 * lax.rem(i, 2) - 1
    return lax.rem(count // 2 + sign * half, count)


def block(index, size):
    return pl.ds(pl.multiple_of(index * size, size), size)


def dot_nt(a, b):
    return lax.dot_general(a, b, (((1,), (1,)), ((), ())), preferred_element_type=F32)


def dot_tn(a, b):
    return lax.dot_general(a, b, (((0,), (0,)), ((), ())), preferred_element_type=F32)


def loop(low, high, step):
    def run(i, carry):
        step(i)
        return carry

    lax.fori_loop(low, high, run, 0)


def layer_kernel(
    planes, groups, cap, stored,
    tok_ref, cot_ref, picks_ref, scale_ref, w_in_ref, w_out_ref,
    mixed_ref, gtok_ref, gin_ref, gout_ref, flag_ref,
    picks_all, maps, ranks, flags, turn, slot_cols, back_cols, tall, pool, hot, packed, pick_hot, got,
    parts, taken, wi, wo, pre, slope, hid, d_pre, msgs, row_hot, home, back_hot, final,
    tins, douts, hids, dpres, rows,
    pick_sem, map_sem, flag_sem, pool_sem, z_sem, part_sem, msg_sem, back_sem, final_sem, x_sem, own_sem,
):
    me = Place(planes, groups)
    z, k, x = me.z, me.k, me.x
    tok, model = tok_ref.shape
    slots = picks_ref.shape[1]
    width = model // PLANE
    n_dev = planes * PLANE
    all_slots = PLANE * slots
    stride = home.shape[1] // planes
    per_group = PLANE // groups
    ffw = hid.shape[1]
    me.greet()

    def pick_copy(d):
        return remote(picks_ref, picks_all.at[k], pick_sem.at[0, d], pick_sem.at[1, d], me.mate(d)[1])

    def pool_copy(which, d):
        spot, peer = me.mate(d)
        return remote(
            (tok_ref, cot_ref)[which].at[:, block(spot, width)],
            pool.at[which, block(k, tok)],
            pool_sem.at[0, which, d], pool_sem.at[1, which, d], peer,
        )

    def map_copy(d):
        spot, peer = me.above(d)
        return remote(maps.at[spot], ranks.at[z], map_sem.at[0, d], map_sem.at[1, d], peer)

    def flag_copy(d):
        return remote(flags.at[x], flags.at[x], flag_sem.at[0, d], flag_sem.at[1, d], me.group(d)[1])

    def z_copy(which, d):
        return remote(
            packed.at[which, d], got.at[which, block(z, cap)],
            z_sem.at[0, which, d], z_sem.at[1, which, d], me.above(d)[1],
        )

    def part_copy(which, d):
        return remote(
            parts.at[which, d], taken.at[which, k],
            part_sem.at[0, which, d], part_sem.at[1, which, d], me.mate(d)[1],
        )

    def msg_copy(which, d):
        return remote(
            parts.at[which, d], msgs.at[which, block(k, slots)],
            msg_sem.at[0, which, d], msg_sem.at[1, which, d], me.mate(d)[1],
        )

    def back_copy(which, d):
        return remote(
            packed.at[which, d],
            home.at[which, pl.ds(pl.multiple_of(z * stride, stride), cap)],
            back_sem.at[0, which, d], back_sem.at[1, which, d], me.above(d)[1],
        )

    def final_copy(which, d):
        return remote(
            final.at[which, d], (mixed_ref, gtok_ref)[which].at[:, block(k, width)],
            final_sem.at[0, which, d], final_sem.at[1, which, d], me.mate(d)[1],
        )

    def x_pair(which, spot):
        src = (
            hid, d_pre, taken.at[0, pl.ds(spot * per_group, per_group)],
            taken.at[1, pl.ds(spot * per_group, per_group)],
        )[which]
        return src, (hids, dpres, tins, douts)[which].at[x]

    def x_copy(which, d):
        spot, peer = me.group(d)
        src, dst = x_pair(which, spot)
        return remote(src, dst, x_sem.at[0, which, d], x_sem.at[1, which, d], peer)

    def x_own(which):
        src, dst = x_pair(which, x)
        return pltpu.make_async_copy(src, dst, own_sem.at[2 + which])

    def x_start(which):
        for d in range(1, groups):
            x_copy(which, d).start()
        x_own(which).start()

    for d in range(1, PLANE):
        pick_copy(d).start()
    for which in range(2):
        for d in range(1, PLANE):
            pool_copy(which, d).start()
    own = [
        pltpu.make_async_copy(
            (tok_ref, cot_ref)[which].at[:, block(k, width)], pool.at[which, block(k, tok)], own_sem.at[which]
        )
        for which in range(2)
    ]
    weights = [
        pltpu.make_async_copy(w_in_ref, wi, own_sem.at[6]),
        pltpu.make_async_copy(w_out_ref, wo, own_sem.at[7]),
    ]
    for copy in own + weights:
        copy.start()
    picks_all[k] = picks_ref[...]
    if stride > cap:
        for which in range(2):
            for p in range(planes):
                home[which, p * stride + cap : (p + 1) * stride] = jnp.zeros((stride - cap, width), BF)
    for d in range(1, PLANE):
        pick_copy(d).wait_recv()

    names = jnp.concatenate([picks_all[i] for i in range(PLANE)], axis=1)
    high, low = names // tok, lax.rem(names, tok)
    high_hot = iota((n_dev, all_slots), 0) == high
    low_hot = one(iota((tok, all_slots), 0) == low)
    tall[...] = low_hot
    need = dot_nt(one(high_hot), low_hot) > 0.5
    need_one = one(need)
    before = one(iota((tok, tok), 0) < iota((tok, tok), 1))
    row_a, row_b = iota((n_dev, n_dev), 0), iota((n_dev, n_dev), 1)
    earlier = one((row_b < row_a) & (row_b // PLANE == row_a // PLANE))
    rank = dot(need_one, before) + jnp.sum(dot(earlier, need_one), axis=1, keepdims=True)
    over = jnp.max(jnp.where(need & (rank > cap - 0.5), 1, 0), axis=(0, 1), keepdims=True)
    ranked = jnp.where(need, rank.astype(I32), -1)
    for p in range(planes):
        maps[p, 0:PLANE] = ranked[p * PLANE : (p + 1) * PLANE]
        maps[p, PLANE : 2 * PLANE] = jnp.broadcast_to(over, (PLANE, tok))
    for d in range(1, planes):
        map_copy(d).start()
    ranks[z] = maps[z]

    rank_hi = jnp.floor(rank * (1.0 / 32.0))
    rank_lo = rank - 32.0 * rank_hi
    found = 32.0 * dot(rank_hi.astype(BF), tall[...]) + dot(rank_lo.astype(BF), tall[...])
    slot_rank = jnp.sum(jnp.where(high_hot, found, 0.0), axis=0, keepdims=True).astype(I32)
    rows[...] = jnp.where(slot_rank < cap, (high // PLANE) * cap + slot_rank, -1)

    for d in range(1, planes):
        map_copy(d).wait_recv()
    flags[x] = jnp.max(ranks[:, PLANE : 2 * PLANE, :], axis=0)
    for d in range(1, groups):
        flag_copy(d).start()

    def pack(which, d, slot):
        rank_map = ranks[lax.rem(z + d, planes), 0:PLANE]
        for h in range(PLANE):
            hot[slot, :, h * tok : (h + 1) * tok] = one(iota((cap, tok), 0) == rank_map[h : h + 1, :])
        return dot(hot[slot], pool[which]).astype(BF)

    for which in range(2):
        own[which].wait()
        for d in range(1, PLANE):
            pool_copy(which, d).wait_recv()

        def send_rows(i, which=which):
            d = far_first(i, planes)
            packed[which, d] = pack(which, d, 0)
            z_copy(which, d).start()

        loop(0, planes - 1, send_rows)
        got[which, block(z, cap)] = pack(which, 0, 1)

    for b in range(all_slots // tok):
        turn[b : b + 1, :] = rows[:, b * tok : (b + 1) * tok].astype(F32)
    turned = turn[...].T.astype(I32)
    per = slots // tok
    for b in range(all_slots // tok):
        slot_cols[b // per, (b % per) * tok : (b % per + 1) * tok] = jnp.broadcast_to(
            turned[:, b : b + 1], (tok, tok)
        )

    def fill_pick(spot, slot):
        pick_hot[slot] = one(iota((slots, planes * cap), 1) == slot_cols[spot][:, 0:1])

    if stored:
        loop(0, PLANE, lambda spot: fill_pick(spot, spot))

    def select_all(which):
        for d in range(1, planes):
            z_copy(which, d).wait_recv()

        def select(d):
            spot = lax.rem(k + d, PLANE)
            if not stored:
                fill_pick(spot, 0)
            return dot(pick_hot[spot if stored else 0], got[which]).astype(BF)

        def send(d):
            parts[which, d] = select(d)
            part_copy(which, d).start()

        loop(1, PLANE, send)
        taken[which, k] = select(0)

    def each_chunk(which, step):
        step(k, True)
        for d in range(1, PLANE):
            part_copy(which, d).wait_recv()
            step(lax.rem(k + PLANE - d, PLANE), False)

    select_all(0)
    for copy in weights:
        copy.wait()

    def project(c, first):
        term = dot(taken[0, c], wi[block(c, width)])
        pre[...] = term if first else pre[...] + term

    each_chunk(0, project)
    x_start(2)
    tile = 32

    def activate(i):
        v = pre[block(i, tile)]
        inner = 0.7978845608028654 * (v + 0.044715 * (v * v * v))
        t = jnp.tanh(inner)
        hid[block(i, tile)] = (0.5 * v * (1.0 + t)).astype(BF)
        bend = 0.7978845608028654 * (1.0 + 0.134145 * (v * v))
        slope[block(i, tile)] = 0.5 * (1.0 + t) + 0.5 * v * ((1.0 - t * t) * bend)

    loop(0, slots // tile, activate)
    x_start(0)
    scale = scale_ref[:, 0:1]

    def contribution(d):
        spot = lax.rem(k + d, PLANE)
        return (scale * dot(hid[...], wo[:, block(spot, width)])).astype(BF)

    def send_contribution(d):
        part_copy(0, d).wait_send()
        parts[0, d] = contribution(d)
        msg_copy(0, d).start()

    loop(1, PLANE, send_contribution)
    msgs[0, block(k, slots)] = contribution(0)

    select_all(1)

    def send_sums(which):
        for d in range(1, PLANE):
            msg_copy(which, d).wait_recv()

        def add_up(d, slot):
            spot = lax.rem(z + d, planes)
            row_hot[slot] = one(iota((cap, all_slots), 0) + spot * cap == rows[...])
            return dot(row_hot[slot], msgs[which]).astype(BF)

        def send(i):
            d = far_first(i, planes)
            z_copy(which, d).wait_send()
            packed[which, d] = add_up(d, 0)
            back_copy(which, d).start()

        loop(0, planes - 1, send)
        home[which, pl.ds(pl.multiple_of(z * stride, stride), cap)] = add_up(0, 1)

    send_sums(0)

    def pull_back(c, first):
        d_out = (scale * taken[1, c].astype(F32)).astype(BF)
        taken[1, c] = d_out
        term = dot_nt(d_out, wo[:, block(c, width)])
        pre[...] = term if first else pre[...] + term

    each_chunk(1, pull_back)

    def chain(i):
        d_pre[block(i, tile)] = (pre[block(i, tile)] * slope[block(i, tile)]).astype(BF)

    loop(0, slots // tile, chain)

    def token_grad(d):
        spot = lax.rem(k + d, PLANE)
        return dot_nt(d_pre[...], wi[block(spot, width)]).astype(BF)

    def send_token_grad(d):
        part_copy(1, d).wait_send()
        parts[1, d] = token_grad(d)
        msg_copy(1, d).start()

    loop(1, PLANE, send_token_grad)
    msgs[1, block(k, slots)] = token_grad(0)
    x_start(1)
    x_start(3)
    send_sums(1)

    for p in range(planes):
        for h in range(PLANE):
            turn[h * planes + p : h * planes + p + 1] = ranks[p, h : h + 1].astype(F32)
    turned_back = turn[...].T.astype(I32)
    for h in range(PLANE):
        back_cols[h, :, 0:planes] = turned_back[:, h * planes : (h + 1) * planes]

    def fill_back(spot, slot):
        cols = back_cols[spot]
        for p in range(planes):
            back_hot[slot, :, p * stride : (p + 1) * stride] = one(
                iota((tok, stride), 1) == cols[:, p : p + 1]
            )

    if stored:
        loop(0, PLANE, lambda spot: fill_back(spot, spot))

    def send_totals(which):
        for d in range(1, planes):
            back_copy(which, d).wait_recv()

        def total(d):
            spot = lax.rem(k + d, PLANE)
            if not stored:
                fill_back(spot, 0)
            final[which, d] = dot(back_hot[spot if stored else 0], home[which]).astype(BF)

        def send(d):
            total(d)
            final_copy(which, d).start()

        loop(1, PLANE, send)
        total(0)
        pltpu.make_async_copy(
            final.at[which, 0], (mixed_ref, gtok_ref)[which].at[:, block(k, width)], own_sem.at[which]
        ).start()

    send_totals(0)
    send_totals(1)

    for which in range(4):
        x_own(which).wait()
        for d in range(1, groups):
            x_copy(which, d).wait_recv()
    for h in range(per_group):
        total_in = dot_tn(tins[0, h], dpres[0])
        for g in range(1, groups):
            total_in += dot_tn(tins[g, h], dpres[g])
        gin_ref[h * width : (h + 1) * width] = total_in.astype(BF)

    def out_grad(m):
        for h in range(per_group):
            total_out = dot_tn(hids[0, :, block(m, width)], douts[0, h])
            for g in range(1, groups):
                total_out += dot_tn(hids[g, :, block(m, width)], douts[g, h])
            gout_ref[block(m, width), h * width : (h + 1) * width] = total_out.astype(BF)

    loop(0, ffw // width, out_grad)

    for d in range(1, groups):
        flag_copy(d).wait()
        for which in range(4):
            x_copy(which, d).wait_send()
    flag_ref[0, 0] = jnp.max(flags[...])
    for which in range(2):
        pltpu.make_async_copy(
            final.at[which, 0], (mixed_ref, gtok_ref)[which].at[:, block(k, width)], own_sem.at[which]
        ).wait()
        for d in range(1, PLANE):
            final_copy(which, d).wait()
            msg_copy(which, d).wait_send()
            pool_copy(which, d).wait_send()
        for d in range(1, planes):
            back_copy(which, d).wait_send()
    for d in range(1, PLANE):
        pick_copy(d).wait_send()
    for d in range(1, planes):
        map_copy(d).wait_send()


def layer(planes, groups, cap, stored, ident, tokens, cotangent, picks, scale, w_in, w_out):
    tok, model = tokens.shape
    slots = picks.shape[1]
    ffw = w_in.shape[1]
    width = model // PLANE
    all_slots = PLANE * slots
    stride = -(-cap // 128) * 128
    per_group = PLANE // groups
    keep = PLANE if stored else 1
    dma = pltpu.SemaphoreType.DMA
    return pl.pallas_call(
        partial(layer_kernel, planes, groups, cap, stored),
        out_shape=(
            jax.ShapeDtypeStruct((tok, model), BF),
            jax.ShapeDtypeStruct((tok, model), BF),
            jax.ShapeDtypeStruct((model // groups, ffw), BF),
            jax.ShapeDtypeStruct((ffw, model // groups), BF),
            jax.ShapeDtypeStruct((1, 1), I32),
        ),
        in_specs=[VMEM] * 4 + [pl.BlockSpec(memory_space=pl.ANY)] * 2,
        out_specs=[VMEM] * 4 + [pl.BlockSpec(memory_space=pltpu.SMEM)],
        scratch_shapes=[
            pltpu.VMEM((PLANE, 1, slots), I32),
            pltpu.VMEM((planes, 2 * PLANE, tok), I32),
            pltpu.VMEM((planes, 2 * PLANE, tok), I32),
            pltpu.VMEM((groups, PLANE, tok), I32),
            pltpu.VMEM((tok, tok), F32),
            pltpu.VMEM((PLANE, slots, tok), I32),
            pltpu.VMEM((PLANE, tok, tok), I32),
            pltpu.VMEM((tok, all_slots), BF),
            pltpu.VMEM((2, PLANE * tok, width), BF),
            pltpu.VMEM((2, cap, PLANE * tok), BF),
            pltpu.VMEM((2, planes, cap, width), BF),
            pltpu.VMEM((keep, slots, planes * cap), BF),
            pltpu.VMEM((2, planes * cap, width), BF),
            pltpu.VMEM((2, PLANE, slots, width), BF),
            pltpu.VMEM((2, PLANE, slots, width), BF),
            pltpu.VMEM(w_in.shape, BF),
            pltpu.VMEM(w_out.shape, BF),
            pltpu.VMEM((slots, ffw), F32),
            pltpu.VMEM((slots, ffw), F32),
            pltpu.VMEM((slots, ffw), BF),
            pltpu.VMEM((slots, ffw), BF),
            pltpu.VMEM((2, all_slots, width), BF),
            pltpu.VMEM((2, cap, all_slots), BF),
            pltpu.VMEM((2, planes * stride, width), BF),
            pltpu.VMEM((keep, tok, planes * stride), BF),
            pltpu.VMEM((2, PLANE, tok, width), BF),
            pltpu.VMEM((groups, per_group, slots, width), BF),
            pltpu.VMEM((groups, per_group, slots, width), BF),
            pltpu.VMEM((groups, slots, ffw), BF),
            pltpu.VMEM((groups, slots, ffw), BF),
            pltpu.VMEM((1, all_slots), I32),
            dma((2, PLANE)),
            dma((2, planes)),
            dma((2, groups)),
            dma((2, 2, PLANE)),
            dma((2, 2, planes)),
            dma((2, 2, PLANE)),
            dma((2, 2, PLANE)),
            dma((2, 2, planes)),
            dma((2, 2, PLANE)),
            dma((2, 4, groups)),
            dma((8,)),
        ],
        compiler_params=pltpu.CompilerParams(
            collective_id=ident, has_side_effects=True, vmem_limit_bytes=LIMIT * 2**20
        ),
        name=f"layer_{cap}",
    )(tokens, cotangent, picks, scale, w_in, w_out)


PIECES = 4


def finish_kernel(count, *refs):
    given, made, held = refs[:count], refs[count : 2 * count], refs[2 * count : 3 * count]
    sems = refs[-1]

    def copy(n, j, out):
        rows = given[n].shape[0] // PIECES
        part = pl.ds(j * rows, rows)
        src, dst = (held[n], made[n]) if out else (given[n], held[n])
        return pltpu.make_async_copy(src.at[part], dst.at[part], sems.at[int(out), n, j])

    spots = [(n, j) for n in range(count) for j in range(PIECES)]
    for n, j in spots:
        copy(n, j, False).start()
    for n, j in spots:
        copy(n, j, False).wait()
        copy(n, j, True).start()
    for n, j in spots:
        copy(n, j, True).wait()


def finish(arrays):
    anywhere = pl.BlockSpec(memory_space=pl.ANY)
    count = len(arrays)
    return pl.pallas_call(
        partial(finish_kernel, count),
        out_shape=tuple(jax.ShapeDtypeStruct(a.shape, a.dtype) for a in arrays),
        in_specs=[anywhere] * count,
        out_specs=[anywhere] * count,
        scratch_shapes=[pltpu.VMEM(a.shape, a.dtype) for a in arrays]
        + [pltpu.SemaphoreType.DMA((2, count, PIECES))],
        name="finish",
    )(*arrays)


def body(tokens, cotangent, picks, valid, comb, w_in, w_out):
    planes = lax.axis_size("expert") // PLANE
    groups = lax.axis_size("dp")
    loose = PLANE * min(tokens.shape[1], PLANE * MOST)
    scale = comb[0, 0] * valid[0, 0].astype(F32)
    scale = jnp.broadcast_to(scale[:, None], (scale.shape[0], 128))
    operands = (tokens[0], cotangent[0], picks[0], scale, w_in[0], w_out[0])
    results = layer(planes, groups, TIGHT, True, 0, *operands)
    results = lax.cond(
        results[4][0, 0] > 0,
        lambda: tuple(layer(planes, groups, loose, False, 1, *operands)[:4]),
        lambda: tuple(results[:4]),
    )
    return tuple(result[None] for result in finish(results))


def solution(mesh):
    placed = (
        P("dp", "expert", None),
        P("dp", "expert", None),
        P("dp", "expert", None),
        P("dp", "expert", None),
        P("dp", "expert", None),
        P("expert", None, None),
        P("expert", None, None),
    )
    return jax.shard_map(
        body,
        mesh=mesh,
        in_specs=placed,
        out_specs=(
            P("dp", "expert", None),
            P("dp", "expert", None),
            P("expert", "dp", None),
            P("expert", None, "dp"),
        ),
        check_vma=False,
    )
```
